32 devices in a mesh: groups: 2 (over y), row: 4 (over z), col: 4 (over x, core).
Axes of the slice: x: 2, y: 2, z: 4, core: 2. Of those that a mesh axis runs over, the one named last changes fastest.
Arguments:
- embeddings: bfloat16 [64, 128, 2560], P(('groups', 'row', 'col')), parts along dimension 0, may hold values from -6 to 6
- proj_weight: bfloat16 [2560, 128], replicated, may hold values from -0.125 to 0.125
- proj_bias: float32 [128], replicated, may hold values from -3 to 3
- bilinear: bfloat16 [128, 256], replicated, may hold values from -0.5 to 0.5
- conv_kernel: float32 [2, 3, 3], replicated, may hold values from -3 to 3
- lengths: int32 [64], P(('groups', 'row', 'col')), parts along dimension 0, may hold values from 32 to 128, as said below
Outputs:
- pooled_maps: float32 [64, 32, 256], P(('groups', 'row'), 'col'), parts along dimension 0
The draws below stay inside these ranges and needn't reach their ends.
There are 2 independent parts, one for each index of `groups`. The reference program is written for one: setup_inputs(seed, part) draws one part's arguments, and reference() takes and returns one part's arrays. A program takes and returns all parts, laid end to end along the dimension named above; an argument that names none is the same for every part. Nothing has to cross between parts.
Inputs may be any that keep to these rules, and one draw needn't show every extreme that they name: `lengths`: every protein has at least 32 residues, and in every draw some protein has exactly 128.
All inputs are finite; a program needn't handle non-finite values.
Results may differ from the reference program's by a relative error of at most 0.005.
Values may be sent and summed in bfloat16 or wider, within the bound.
A program may use at most 64 MiB of HBM per device.

```python
import jax
import jax.numpy as jnp
from jax import lax

E = 2560
P_SIZE = 128
H = 2
POOL = 8
L = 128
NPROT = 32


def draw_lengths(key, part):
    key = jax.random.fold_in(key, 11)
    first_key, second_key = jax.random.split(key)
    drawn = jax.random.randint(first_key, (NPROT,), L // 4, L + 1, dtype=jnp.int32)
    longest = jax.random.randint(second_key, (), 0, NPROT, dtype=jnp.int32)
    return drawn.at[longest].set(L)


def block_levels(key, shape, pieces, smallest, high):
    def one(dim, blocks):
        heights = jax.random.uniform(jax.random.fold_in(jax.random.fold_in(key, 6), dim), (blocks,), jnp.float32, smallest / len(pieces), high / len(pieces))
        return jnp.repeat(jnp.exp(heights), shape[dim] // blocks).reshape((-1,) + (1,) * (len(shape) - dim - 1))

    loudness = one(*pieces[0])
    for cut in pieces[1:]:
        loudness = loudness * one(*cut)
    return loudness


def noise(key, shape, scale, reach, pieces=(), kind=jnp.bfloat16):
    entries = jax.random.normal(key, shape, jnp.float32) * scale
    if len(pieces) > 0:
        entries = block_levels(key, shape, pieces, -0.22, 0.18) * entries
    return jnp.clip(entries, min=-reach, max=reach).astype(kind)


def setup_inputs(seed: int = 0, part: int = 0) -> dict:
    arg_keys = jax.random.split(jax.random.key(seed), 7)
    own_keys = jax.random.split(jax.random.fold_in(arg_keys[6], part), 7)
    return {
        "embeddings": noise(own_keys[0], (NPROT, L, E), 1.0, 6.0, ((0, 16),)),
        "proj_weight": noise(arg_keys[1], (E, P_SIZE), E ** -0.5, 0.125),
        "proj_bias": noise(arg_keys[2], (P_SIZE,), 0.5, 3.0, (), jnp.float32),
        "bilinear": noise(arg_keys[3], (P_SIZE, H * P_SIZE), P_SIZE ** -0.5, 0.5),
        "conv_kernel": noise(arg_keys[4], (H, 3, 3), 0.5, 3.0, (), jnp.float32),
        "lengths": draw_lengths(jax.random.fold_in(jax.random.fold_in(arg_keys[6], part), 71), part),
    }


def fold_images(mapped_block, kernel):
    count, extent, wide = mapped_block.shape
    channels = kernel.shape[0]
    proj_width = wide // channels
    padded = jnp.pad(mapped_block.astype(jnp.float32), ((0, 0), (1, 1), (0, 0)))
    stacked = []
    for offset_a in range(3):
        total = jnp.zeros((count, extent, proj_width), jnp.float32)
        for channel in range(channels):
            for offset_b in range(3):
                total = total + kernel[channel, offset_a, offset_b] * padded[:, offset_b:offset_b + extent, channel * proj_width:(channel + 1) * proj_width]
        stacked.append(total)
    return jnp.concatenate(stacked, axis=2).astype(jnp.bfloat16)


def shifted_rows(res_block):
    extent = res_block.shape[1]
    padded = jnp.pad(res_block, ((0, 0), (1, 1), (0, 0)))
    return jnp.concatenate([padded[:, 0:extent], padded[:, 1:extent + 1], padded[:, 2:extent + 2]], axis=2)


def pair_maps(row_stack, row_len, col_folded, col_len):
    extent = row_stack.shape[0]
    proj_width = row_stack.shape[1] // 3
    columns = col_folded.shape[0]
    contact = jnp.einsum('aq,nbq->nab', row_stack.astype(jnp.float32), col_folded.astype(jnp.float32)) * (proj_width ** -0.5)
    positions = jnp.arange(extent, dtype=jnp.int32)
    row_valid = (positions < row_len).astype(jnp.float32)
    col_valid = (positions[None, :] < col_len[:, None]).astype(jnp.float32)
    result = contact * (row_valid[None, :, None] * col_valid[:, None, :])
    cell_count = extent // POOL
    pooled = result.reshape(columns, cell_count, POOL, cell_count, POOL).max(axis=(2, 4))
    return pooled.reshape(columns, cell_count * cell_count)


def reference(embeddings, proj_weight, proj_bias, bilinear, conv_kernel, lengths):
    protein_count = embeddings.shape[0]
    positions = jnp.arange(L, dtype=jnp.int32)
    valid = (positions[None, :] < lengths[:, None]).astype(jnp.float32)
    flattened = embeddings.reshape(protein_count * L, E)
    raw = jax.nn.relu(jnp.dot(flattened, proj_weight, preferred_element_type=jnp.float32) + proj_bias)
    residues = (raw.reshape(protein_count, L, P_SIZE) * valid[:, :, None]).astype(jnp.bfloat16)
    mapped = jnp.dot(residues.reshape(protein_count * L, P_SIZE), bilinear, preferred_element_type=jnp.float32).astype(jnp.bfloat16)
    mapped = mapped.reshape(protein_count, L, H * P_SIZE)
    folded = fold_images(mapped, conv_kernel)
    stacks = shifted_rows(residues)
    protein_ids = jnp.arange(protein_count, dtype=jnp.int32)

    def one_row(element):
        row_stack, row_len, row_id = element
        pooled = pair_maps(row_stack, row_len, folded, lengths)
        return jnp.where((protein_ids > row_id)[:, None], pooled, jnp.zeros_like(pooled))

    return lax.map(one_row, (stacks, lengths, protein_ids))
```

```python
import functools

import jax
import jax.numpy as jnp
from jax import lax
from jax.experimental import pallas as pl
from jax.experimental.pallas import tpu as pltpu
from jax.sharding import PartitionSpec as P

POOL = 8
GROUP = 8
MESH = pl.DeviceIdType.MESH
CHUNKS = 4


def kernel(
    rows,
    cols,
    owned,
    cells,
    lens_ref,
    conv_ref,
    bias_ref,
    bil_hbm,
    emb_hbm,
    w_hbm,
    out_ref,
    emb,
    w,
    bil,
    mine,
    my_len,
    row_buf,
    col_buf,
    row_len,
    col_len,
    stack_w,
    row_stack,
    col_stack,
    folded,
    load_sem,
    row_send,
    row_recv,
    col_send,
    col_recv,
    rl_send,
    rl_recv,
    cl_send,
    cl_recv,
):
    f32, bf16 = jnp.float32, jnp.bfloat16
    extent = cells * POOL
    width = bil.shape[0]
    g = lax.axis_index("groups")
    r = lax.axis_index("row")
    c = lax.axis_index("col")
    flat = r * cols + c
    my_block = flat // rows
    my_slot = flat % rows

    def active(row, col):
        return (col + 1) * rows * owned > row * cols * owned + 1

    def one(flag):
        return jnp.where(flag, 1, 0)

    here = active(r, c)

    depth = emb_hbm.shape[1] // CHUNKS
    loads = []
    for n in range(CHUNKS):
        span = pl.ds(n * depth, depth)
        pair = (
            pltpu.make_async_copy(emb_hbm.at[:, span], emb.at[n], load_sem.at[2 * n]),
            pltpu.make_async_copy(w_hbm.at[span, :], w.at[n], load_sem.at[2 * n + 1]),
        )
        for copy in pair:
            copy.start()
        loads.append(pair)
    bil_load = pltpu.make_async_copy(bil_hbm, bil, load_sem.at[2 * CHUNKS])
    bil_load.start()

    row_peers = [lax.rem(c + d, cols) for d in range(1, cols)]
    col_peers = [lax.rem(r + d, rows) for d in range(rows)]

    def col_remote(row):
        same = jnp.logical_and(row == r, my_block == c)
        return jnp.logical_and(active(row, my_block), jnp.logical_not(same))

    barrier = pltpu.get_barrier_semaphore()
    for peer in row_peers:

        @pl.when(here)
        def _():
            pl.semaphore_signal(barrier, inc=1, device_id=(g, r, peer), device_id_type=MESH)

    for slot in range(rows):
        source = c * rows + slot

        @pl.when(jnp.logical_and(here, source != flat))
        def _():
            pl.semaphore_signal(
                barrier, inc=1, device_id=(g, source // cols, source % cols), device_id_type=MESH
            )

    my_len[...] = jnp.zeros_like(my_len)
    for p in range(owned):
        my_len[p : p + 1, :] = jnp.full((1, my_len.shape[1]), lens_ref[p], jnp.int32)

    sends = 0
    for peer in row_peers:
        sends = sends + one(active(r, peer))
    for peer in col_peers:
        sends = sends + one(col_remote(peer))
    pl.semaphore_wait(barrier, sends)

    def row_copies(n, peer):
        to = dict(device_id=(g, r, peer), device_id_type=MESH)
        return (
            pltpu.make_async_remote_copy(
                src_ref=my_len, dst_ref=row_len.at[c], send_sem=rl_send.at[n], recv_sem=rl_recv.at[c], **to
            ),
            pltpu.make_async_remote_copy(
                src_ref=mine,
                dst_ref=row_buf.at[:, pl.ds(c * owned, owned)],
                send_sem=row_send.at[n],
                recv_sem=row_recv.at[c],
                **to,
            ),
        )

    def col_copies(n, peer):
        to = dict(device_id=(g, peer, my_block), device_id_type=MESH)
        return (
            pltpu.make_async_remote_copy(
                src_ref=my_len,
                dst_ref=col_len.at[my_slot],
                send_sem=cl_send.at[n],
                recv_sem=cl_recv.at[my_slot],
                **to,
            ),
            pltpu.make_async_remote_copy(
                src_ref=mine,
                dst_ref=col_buf.at[:, pl.ds(my_slot * owned, owned)],
                send_sem=col_send.at[n],
                recv_sem=col_recv.at[my_slot],
                **to,
            ),
        )

    outgoing = [(active(r, peer), row_copies(n, peer)) for n, peer in enumerate(row_peers)]
    outgoing = [
        (col_remote(peer), col_copies(n, peer)) for n, peer in enumerate(col_peers)
    ][::-1] + outgoing
    for flag, copies in outgoing:

        @pl.when(flag)
        def _():
            copies[0].start()

    total = jnp.zeros((owned * extent, width), f32)
    for n, pair in enumerate(loads):
        for copy in pair:
            copy.wait()
        total = total + jnp.dot(emb[n], w[n], preferred_element_type=f32)
    place = lax.broadcasted_iota(jnp.int32, (owned * extent, width), 0)
    limit = jnp.zeros((owned * extent, width), jnp.int32)
    for p in range(owned):
        limit = jnp.where(place // extent == p, lens_ref[p] + p * extent, limit)
    total = jnp.maximum(total + bias_ref[...][None, :], 0.0)
    residues = jnp.where(place < limit, total, 0.0).astype(bf16)
    size = owned * extent
    to_row = lax.broadcasted_iota(jnp.int32, (size, size), 0)
    from_row = lax.broadcasted_iota(jnp.int32, (size, size), 1)
    k_of = to_row // (owned * cells)
    rest = to_row % (owned * cells)
    wanted = (rest // cells) * extent + (rest % cells) * POOL + k_of
    order = jnp.where(wanted == from_row, 1.0, 0.0).astype(bf16)
    ordered = jnp.dot(order, residues, preferred_element_type=f32).astype(bf16)
    mine[...] = ordered.reshape(POOL, owned, cells, width)

    for flag, copies in outgoing:

        @pl.when(flag)
        def _():
            copies[1].start()

    def shifted(slab, step):
        count = slab.shape[0]
        wide = slab.astype(f32)
        cell = lax.broadcasted_iota(jnp.int32, wide.shape, 0) % cells
        if step > 0:
            moved = jnp.where(cell == cells - 1, 0.0, pltpu.roll(wide, count - 1, 0))
        else:
            moved = jnp.where(cell == 0, 0.0, pltpu.roll(wide, 1, 0))
        return moved.astype(bf16)

    def masks(lens, base):
        parts = []
        for i in range(GROUP):
            parts.append(
                jnp.broadcast_to(lens[(base + i) // owned, (base + i) % owned][None, :], (cells, width))
            )
        limits = jnp.concatenate(parts, axis=0)
        first = (lax.broadcasted_iota(jnp.int32, limits.shape, 0) % cells) * POOL
        return [jnp.where(first + k < limits, 1.0, 0.0) for k in range(POOL)]

    def build(buf, base, k):
        def slab(index):
            return buf[index, pl.ds(base, GROUP)].reshape(GROUP * cells, width)

        before = slab(k - 1) if k > 0 else shifted(slab(POOL - 1), -1)
        after = slab(k + 1) if k < POOL - 1 else shifted(slab(0), 1)
        return before, slab(k), after

    bil_load.wait()

    @pl.when(here)
    def _():
        channels = conv_ref.shape[0]
        for u in range(3):
            for v in range(3):
                form = jnp.zeros((width, width), f32)
                for h in range(channels):
                    form = form + (conv_ref[h, u, v] * width ** (-0.5)) * bil[
                        :, h * width : (h + 1) * width
                    ].astype(f32)
                stack_w[v * width : (v + 1) * width, u * width : (u + 1) * width] = form.astype(bf16)

        row_buf[:, pl.ds(c * owned, owned)] = mine[...]
        row_len[c] = my_len[...]

        @pl.when(my_block == c)
        def _():
            col_buf[:, pl.ds(my_slot * owned, owned)] = mine[...]
            col_len[my_slot] = my_len[...]

        for d in range(1, cols):
            peer = lax.rem(c + cols - d, cols)
            for pair in (
                (row_len.at[peer], rl_recv.at[peer]),
                (row_buf.at[:, pl.ds(peer * owned, owned)], row_recv.at[peer]),
            ):
                pltpu.make_async_copy(pair[0], pair[0], pair[1]).wait()

        row_mask = masks(row_len, 0)
        for k in range(POOL):
            parts = build(row_buf, 0, k)
            keep = row_mask[k].astype(bf16)
            for u in range(3):
                row_stack[k * GROUP * cells : (k + 1) * GROUP * cells, u * width : (u + 1) * width] = (
                    parts[u] * keep
                )

        for slot in range(rows):

            @pl.when(c * rows + slot != flat)
            def _():
                for pair in (
                    (col_len.at[slot], cl_recv.at[slot]),
                    (col_buf.at[:, pl.ds(slot * owned, owned)], col_recv.at[slot]),
                ):
                    pltpu.make_async_copy(pair[0], pair[0], pair[1]).wait()

        high = GROUP * cells
        for chunk in range(rows * owned // GROUP):
            base = chunk * GROUP
            col_mask = masks(col_len, base)
            for k in range(POOL):
                parts = build(col_buf, base, k)
                for v in range(3):
                    col_stack[k * high : (k + 1) * high, v * width : (v + 1) * width] = parts[v]
            for k in range(POOL):
                image = jnp.dot(
                    col_stack[k * high : (k + 1) * high, :], stack_w[...], preferred_element_type=f32
                )
                keep = jnp.concatenate([col_mask[k]] * 3, axis=1)
                folded[k * high : (k + 1) * high, :] = (image * keep).astype(bf16)
            best = None
            for step in range(POOL // 2):
                contact = lax.dot_general(
                    row_stack[...],
                    folded[step * 2 * high : (step + 1) * 2 * high, :],
                    (((1,), (1,)), ((), ())),
                    preferred_element_type=f32,
                )
                for k in range(POOL):
                    for half in range(2):
                        part = contact[k * high : (k + 1) * high, half * high : (half + 1) * high]
                        best = part if best is None else jnp.maximum(best, part)
            sub = lax.broadcasted_iota(jnp.int32, best.shape, 0) % 8
            lane = lax.broadcasted_iota(jnp.int32, best.shape, 1) // cells
            for bit in (1, 2, 4):
                down = pltpu.roll(pltpu.roll(best, bit, 0), high - bit * cells, 1)
                up = pltpu.roll(pltpu.roll(best, high - bit, 0), bit * cells, 1)
                s_on = (sub & bit) != 0
                l_on = (lane & bit) != 0
                best = jnp.where(s_on == l_on, best, jnp.where(s_on, down, up))
            halves = cells // 8
            tiles = best.reshape(GROUP, halves, GROUP, high)
            j_id = c * rows * owned + base + lax.broadcasted_iota(jnp.int32, (GROUP, high), 0)
            for i in range(GROUP):
                keep = j_id > r * cols * owned + i
                for half in range(halves):
                    out_ref[i, pl.ds(base, GROUP), half * high : (half + 1) * high] = jnp.where(
                        keep, tiles[i, half], 0.0
                    )

    @pl.when(jnp.logical_not(here))
    def _():
        out_ref[...] = jnp.zeros_like(out_ref)

    for flag, copies in outgoing:

        @pl.when(flag)
        def _():
            for copy in copies:
                copy.wait_send()


def shards(rows, cols, embeddings, proj_weight, proj_bias, bilinear, conv_kernel, lengths):
    owned, extent, embed = embeddings.shape
    width = proj_weight.shape[1]
    cells = extent // POOL
    assert owned * cols == GROUP and (owned * rows) % GROUP == 0
    assert extent == width == GROUP * cells
    bf16, f32 = jnp.bfloat16, jnp.float32
    dma = pltpu.SemaphoreType.DMA
    high = POOL * GROUP * cells
    return pl.pallas_call(
        functools.partial(kernel, rows, cols, owned, cells),
        out_shape=jax.ShapeDtypeStruct((owned * cols, owned * rows, cells * cells), f32),
        in_specs=[
            pl.BlockSpec(memory_space=pltpu.SMEM),
            pl.BlockSpec(memory_space=pltpu.SMEM),
            pl.BlockSpec(memory_space=pltpu.VMEM),
            pl.BlockSpec(memory_space=pl.ANY),
            pl.BlockSpec(memory_space=pl.ANY),
            pl.BlockSpec(memory_space=pl.ANY),
        ],
        out_specs=pl.BlockSpec(memory_space=pltpu.VMEM),
        scratch_shapes=[
            pltpu.VMEM((CHUNKS, owned * extent, embed // CHUNKS), bf16),
            pltpu.VMEM((CHUNKS, embed // CHUNKS, width), bf16),
            pltpu.VMEM(bilinear.shape, bf16),
            pltpu.VMEM((POOL, owned, cells, width), bf16),
            pltpu.VMEM((8, width), jnp.int32),
            pltpu.VMEM((POOL, owned * cols, cells, width), bf16),
            pltpu.VMEM((POOL, owned * rows, cells, width), bf16),
            pltpu.VMEM((cols, 8, width), jnp.int32),
            pltpu.VMEM((rows, 8, width), jnp.int32),
            pltpu.VMEM((3 * width, 3 * width), bf16),
            pltpu.VMEM((high, 3 * width), bf16),
            pltpu.VMEM((high, 3 * width), bf16),
            pltpu.VMEM((high, 3 * width), bf16),
            dma((2 * CHUNKS + 1,)),
            dma((cols,)),
            dma((cols,)),
            dma((rows,)),
            dma((rows,)),
            dma((cols,)),
            dma((cols,)),
            dma((rows,)),
            dma((rows,)),
        ],
        compiler_params=pltpu.CompilerParams(
            collective_id=0, has_side_effects=True, vmem_limit_bytes=48 * 1024 * 1024
        ),
    )(
        lengths,
        conv_kernel,
        proj_bias,
        bilinear,
        embeddings.reshape(owned * extent, embed),
        proj_weight,
    )


def solution(mesh):
    in_specs = (
        P(("groups", "row", "col"), None, None),
        P(),
        P(),
        P(),
        P(),
        P(("groups", "row", "col")),
    )
    out_specs = P(("groups", "row"), "col", None)
    body = functools.partial(shards, mesh.shape["row"], mesh.shape["col"])
    return jax.shard_map(body, mesh=mesh, in_specs=in_specs, out_specs=out_specs, check_vma=False)
```

```python
import functools

import jax
import jax.numpy as jnp
from jax import lax
from jax.experimental import pallas as pl
from jax.experimental.pallas import tpu as pltpu
from jax.sharding import PartitionSpec as P

POOL = 8
GROUP = 8
MESH = pl.DeviceIdType.MESH
CHUNKS = 4


def shifted(slab, step, cells):
    count = slab.shape[0]
    wide = slab.astype(jnp.float32)
    cell = lax.broadcasted_iota(jnp.int32, wide.shape, 0) % cells
    if step > 0:
        moved = jnp.where(cell == cells - 1, 0.0, pltpu.roll(wide, count - 1, 0))
    else:
        moved = jnp.where(cell == 0, 0.0, pltpu.roll(wide, 1, 0))
    return moved.astype(jnp.bfloat16)


def masks(lens, base, owned, cells, width):
    parts = []
    for i in range(GROUP):
        parts.append(
            jnp.broadcast_to(lens[(base + i) // owned, (base + i) % owned][None, :], (cells, width))
        )
    limits = jnp.concatenate(parts, axis=0)
    first = (lax.broadcasted_iota(jnp.int32, limits.shape, 0) % cells) * POOL
    return [jnp.where(first + k < limits, 1.0, 0.0) for k in range(POOL)]


def build(buf, base, k, owned, cells, width):
    def slab(index):
        return buf[pl.ds(base // owned, GROUP // owned), index].reshape(GROUP * cells, width)

    before = slab(k - 1) if k > 0 else shifted(slab(POOL - 1), -1, cells)
    after = slab(k + 1) if k < POOL - 1 else shifted(slab(0), 1, cells)
    return before, slab(k), after


def merge_taps(conv_ref, bil, stack_w, width):
    channels = conv_ref.shape[1]
    for u in range(3):
        for v in range(3):
            form = jnp.zeros((width, width), jnp.float32)
            for h in range(channels):
                form = form + (conv_ref[u, h, v] * width ** (-0.5)) * bil[
                    :, h * width : (h + 1) * width
                ].astype(jnp.float32)
            stack_w[v * width : (v + 1) * width, u * width : (u + 1) * width] = form.astype(jnp.bfloat16)


def fill_rows(buf, lens, row_stack, owned, cells, width):
    high = GROUP * cells
    row_mask = masks(lens, 0, owned, cells, width)
    for k in range(POOL):
        parts = build(buf, 0, k, owned, cells, width)
        keep = row_mask[k].astype(jnp.bfloat16)
        for u in range(3):
            row_stack[k * high : (k + 1) * high, u * width : (u + 1) * width] = parts[u] * keep


def fill_cols(buf, lens, base, stack_w, col_stack, folded, owned, cells, width):
    high = GROUP * cells
    col_mask = masks(lens, base, owned, cells, width)
    for k in range(POOL):
        parts = build(buf, base, k, owned, cells, width)
        for v in range(3):
            col_stack[k * high : (k + 1) * high, v * width : (v + 1) * width] = parts[v]
    for k in range(POOL):
        image = jnp.dot(
            col_stack[k * high : (k + 1) * high, :], stack_w[...], preferred_element_type=jnp.float32
        )
        keep = jnp.concatenate([col_mask[k]] * 3, axis=1)
        folded[k * high : (k + 1) * high, :] = (image * keep).astype(jnp.bfloat16)


def pair_tiles(row_stack, folded, cells):
    high = GROUP * cells
    best = None
    for step in range(POOL // 2):
        contact = lax.dot_general(
            row_stack[...],
            folded[step * 2 * high : (step + 1) * 2 * high, :],
            (((1,), (1,)), ((), ())),
            preferred_element_type=jnp.float32,
        )
        for k in range(POOL):
            for half in range(2):
                part = contact[k * high : (k + 1) * high, half * high : (half + 1) * high]
                best = part if best is None else jnp.maximum(best, part)
    sub = lax.broadcasted_iota(jnp.int32, best.shape, 0) % 8
    lane = lax.broadcasted_iota(jnp.int32, best.shape, 1) // cells
    for bit in (1, 2, 4):
        down = pltpu.roll(pltpu.roll(best, bit, 0), high - bit * cells, 1)
        up = pltpu.roll(pltpu.roll(best, high - bit, 0), bit * cells, 1)
        s_on = (sub & bit) != 0
        l_on = (lane & bit) != 0
        best = jnp.where(s_on == l_on, best, jnp.where(s_on, down, up))
    return best.reshape(GROUP, cells // 8, GROUP, high)


def start_loads(refs, load_sem):
    lens_hbm, conv_hbm, bias_hbm, bil_hbm, emb_hbm, w_hbm, emb, w, bil, lens_ref, conv_ref, bias_ref = refs
    small = [
        pltpu.make_async_copy(src, dst, load_sem.at[2 * CHUNKS + n])
        for n, (src, dst) in enumerate(
            ((lens_hbm, lens_ref), (bias_hbm, bias_ref), (bil_hbm, bil), (conv_hbm, conv_ref))
        )
    ]
    small[0].start()
    depth = emb_hbm.shape[1] // CHUNKS
    loads = []
    for n in range(CHUNKS):
        span = pl.ds(n * depth, depth)
        pair = (
            pltpu.make_async_copy(emb_hbm.at[:, span], emb.at[n], load_sem.at[2 * n]),
            pltpu.make_async_copy(w_hbm.at[span, :], w.at[n], load_sem.at[2 * n + 1]),
        )
        for copy in pair:
            copy.start()
        loads.append(pair)
    for copy in small[1:]:
        copy.start()
    return small, loads


def make_order(order, owned, cells):
    extent, size = cells * POOL, owned * cells * POOL
    to_row = lax.broadcasted_iota(jnp.int32, (size, size), 0)
    from_row = lax.broadcasted_iota(jnp.int32, (size, size), 1)
    k_of = to_row // (owned * cells)
    rest = to_row % (owned * cells)
    wanted = (rest // cells) * extent + (rest % cells) * POOL + k_of
    order[...] = jnp.where(wanted == from_row, 1.0, 0.0).astype(jnp.bfloat16)


def project(loads, small, emb, w, lens_ref, bias_ref, order, mine, owned, cells):
    f32, bf16 = jnp.float32, jnp.bfloat16
    extent, width = cells * POOL, w.shape[2]
    small[1].wait()
    total = jnp.zeros((owned * extent, width), f32)
    for n, pair in enumerate(loads):
        for copy in pair:
            copy.wait()
        total = total + jnp.dot(emb[n], w[n], preferred_element_type=f32)
    place = lax.broadcasted_iota(jnp.int32, (owned * extent, width), 0)
    limit = jnp.zeros((owned * extent, width), jnp.int32)
    for p in range(owned):
        limit = jnp.where(place // extent == p, lens_ref[p] + p * extent, limit)
    total = jnp.maximum(total + bias_ref[...][None, :], 0.0)
    residues = jnp.where(place < limit, total, 0.0).astype(bf16)
    ordered = jnp.dot(order[...], residues, preferred_element_type=f32).astype(bf16)
    mine[...] = ordered.reshape(POOL, owned, cells, width)


def fill_len(small, lens_ref, my_len, owned):
    small[0].wait()
    my_len[...] = jnp.zeros_like(my_len)
    for p in range(owned):
        my_len[p : p + 1, :] = jnp.full((1, my_len.shape[1]), lens_ref[p], jnp.int32)


def square_kernel(
    size, owned, cells, lens_hbm, conv_hbm, bias_hbm, bil_hbm, emb_hbm, w_hbm, out_ref,
    emb, w, bil, lens_ref, conv_ref, bias_ref, order, mine, my_len, buf, lens,
    stack_w, row_stack, col_stack, folded,
    load_sem, home_send, away_send, recv, len_home_send, len_away_send, len_recv, relay_send,
):
    width = bil.shape[0]
    g = lax.axis_index("groups")
    a = lax.axis_index("row")
    b = lax.axis_index("col")

    def one(flag):
        return jnp.where(flag, 1, 0)

    def twin(col):
        return col + 1 - 2 * (col % 2)

    def active(row, col):
        return row <= col

    def carries(row, col):
        return jnp.logical_or(active(row, col), active(row, twin(col)))

    here = active(a, b)
    other = twin(b)
    small, loads = start_loads(
        (lens_hbm, conv_hbm, bias_hbm, bil_hbm, emb_hbm, w_hbm, emb, w, bil, lens_ref, conv_ref, bias_ref),
        load_sem,
    )
    homes = [lax.rem(b + d, size) for d in range(1, size)]
    aways = [lax.rem(a + d, size) for d in range(1, size)]
    crosses = []

    barrier = pltpu.get_barrier_semaphore()

    def greet(row, col):
        pl.semaphore_signal(barrier, inc=1, device_id=(g, row, col), device_id_type=MESH)

    for peer in homes:
        greet(a, peer)

    @pl.when(a < b)
    def _():
        for peer in range(size):
            greet(b, peer)

    make_order(order, owned, cells)
    fill_len(small, lens_ref, my_len, owned)
    sends = size - 1
    for peer in aways:
        sends = sends + one(peer < a)
    pl.semaphore_wait(barrier, sends)

    def length_copy(kind, n, row, col):
        return pltpu.make_async_remote_copy(
            src_ref=my_len,
            dst_ref=lens.at[kind, b],
            send_sem=(len_home_send, len_away_send)[kind].at[n],
            recv_sem=len_recv.at[kind, b],
            device_id=(g, row, col),
            device_id_type=MESH,
        )

    def residue_copy(kind, n, row, col):
        return pltpu.make_async_remote_copy(
            src_ref=mine,
            dst_ref=buf.at[kind, b],
            send_sem=(home_send, away_send)[kind].at[n],
            recv_sem=recv.at[kind, b],
            device_id=(g, row, col),
            device_id_type=MESH,
        )

    def relay_copy(n, source):
        place = buf.at[0, source]
        return pltpu.make_async_remote_copy(
            src_ref=place,
            dst_ref=place,
            send_sem=relay_send.at[n],
            recv_sem=recv.at[0, source],
            device_id=(g, a, other),
            device_id_type=MESH,
        )

    len_out = [(active(a, peer), length_copy(0, n, a, peer)) for n, peer in enumerate(homes)]
    len_out += [(peer < a, length_copy(1, n, peer, a)) for n, peer in enumerate(aways)]
    away_out = [(peer < a, residue_copy(1, n, peer, a)) for n, peer in enumerate(aways)]
    home_out = [(carries(a, peer), residue_copy(0, n, a, peer)) for n, peer in enumerate(crosses)]
    home_out = [(active(a, peer), residue_copy(0, n, a, peer)) for n, peer in enumerate(homes)]

    def start(group):
        for flag, copy in group:

            @pl.when(flag)
            def _():
                copy.start()

    start(len_out)
    project(loads, small, emb, w, lens_ref, bias_ref, order, mine, owned, cells)
    start(home_out)
    start(away_out)
    small[2].wait()
    small[3].wait()

    @pl.when(here)
    def _():
        merge_taps(conv_ref, bil, stack_w, width)
        buf[0, b] = mine[...]
        lens[0, b] = my_len[...]

    def landed(kind, source):
        ref = buf.at[kind, source]
        pltpu.make_async_copy(ref, ref, recv.at[kind, source]).wait()

    def len_landed(kind, source):
        ref = lens.at[kind, source]
        pltpu.make_async_copy(ref, ref, len_recv.at[kind, source]).wait()

    relays = [(active(a, other), relay_copy(n, peer)) for n, peer in enumerate(crosses)]
    for peer, item in zip(crosses, relays):

        @pl.when(carries(a, b))
        def _():
            landed(0, peer)

        start([item])

    @pl.when(here)
    def _():
        for peer in homes:
            len_landed(0, peer)
        for peer in homes:
            landed(0, peer)
        fill_rows(buf.at[0], lens.at[0], row_stack, owned, cells, width)

        @pl.when(a != b)
        def _():
            for source in range(size):
                len_landed(1, source)
                landed(1, source)

        kind = one(a != b)
        fill_cols(buf.at[kind], lens.at[kind], 0, stack_w, col_stack, folded, owned, cells, width)
        found = pair_tiles(row_stack, folded, cells)
        halves, high = found.shape[1], found.shape[3]
        j_id = b * size * owned + lax.broadcasted_iota(jnp.int32, (GROUP, high), 0)
        for i in range(GROUP):
            keep = j_id > a * size * owned + i
            for half in range(halves):
                tile = jnp.where(keep, found[i, half], 0.0)
                out_ref[i, :, half * high : (half + 1) * high] = tile

    @pl.when(jnp.logical_not(here))
    def _():
        out_ref[...] = jnp.zeros_like(out_ref)

    for flag, copy in len_out + away_out + home_out + relays:

        @pl.when(flag)
        def _():
            copy.wait_send()


def kernel(
    rows,
    cols,
    owned,
    cells,
    lens_hbm,
    conv_hbm,
    bias_hbm,
    bil_hbm,
    emb_hbm,
    w_hbm,
    out_ref,
    emb,
    w,
    bil,
    lens_ref,
    conv_ref,
    bias_ref,
    order,
    mine,
    my_len,
    row_buf,
    col_buf,
    row_len,
    col_len,
    stack_w,
    row_stack,
    col_stack,
    folded,
    load_sem,
    row_send,
    row_recv,
    col_send,
    col_recv,
    rl_send,
    rl_recv,
    cl_send,
    cl_recv,
):
    width = bil.shape[0]
    g = lax.axis_index("groups")
    r = lax.axis_index("row")
    c = lax.axis_index("col")
    flat = r * cols + c
    my_block = flat // rows
    my_slot = flat % rows

    def active(row, col):
        return (col + 1) * rows * owned > row * cols * owned + 1

    def one(flag):
        return jnp.where(flag, 1, 0)

    here = active(r, c)

    small, loads = start_loads(
        (lens_hbm, conv_hbm, bias_hbm, bil_hbm, emb_hbm, w_hbm, emb, w, bil, lens_ref, conv_ref, bias_ref),
        load_sem,
    )

    row_peers = [lax.rem(c + d, cols) for d in range(1, cols)]
    col_peers = [lax.rem(r + d, rows) for d in range(rows)]

    def col_remote(row):
        same = jnp.logical_and(row == r, my_block == c)
        return jnp.logical_and(active(row, my_block), jnp.logical_not(same))

    barrier = pltpu.get_barrier_semaphore()
    for peer in row_peers:

        @pl.when(here)
        def _():
            pl.semaphore_signal(barrier, inc=1, device_id=(g, r, peer), device_id_type=MESH)

    for slot in range(rows):
        source = c * rows + slot

        @pl.when(jnp.logical_and(here, source != flat))
        def _():
            pl.semaphore_signal(
                barrier, inc=1, device_id=(g, source // cols, source % cols), device_id_type=MESH
            )

    make_order(order, owned, cells)
    fill_len(small, lens_ref, my_len, owned)
    sends = 0
    for peer in row_peers:
        sends = sends + one(active(r, peer))
    for peer in col_peers:
        sends = sends + one(col_remote(peer))
    pl.semaphore_wait(barrier, sends)

    def row_copies(n, peer):
        to = dict(device_id=(g, r, peer), device_id_type=MESH)
        return (
            pltpu.make_async_remote_copy(
                src_ref=my_len, dst_ref=row_len.at[c], send_sem=rl_send.at[n], recv_sem=rl_recv.at[c], **to
            ),
            pltpu.make_async_remote_copy(
                src_ref=mine,
                dst_ref=row_buf.at[c],
                send_sem=row_send.at[n],
                recv_sem=row_recv.at[c],
                **to,
            ),
        )

    def col_copies(n, peer):
        to = dict(device_id=(g, peer, my_block), device_id_type=MESH)
        return (
            pltpu.make_async_remote_copy(
                src_ref=my_len,
                dst_ref=col_len.at[my_slot],
                send_sem=cl_send.at[n],
                recv_sem=cl_recv.at[my_slot],
                **to,
            ),
            pltpu.make_async_remote_copy(
                src_ref=mine,
                dst_ref=col_buf.at[my_slot],
                send_sem=col_send.at[n],
                recv_sem=col_recv.at[my_slot],
                **to,
            ),
        )

    outgoing = [(active(r, peer), row_copies(n, peer)) for n, peer in enumerate(row_peers)]
    outgoing = [
        (col_remote(peer), col_copies(n, peer)) for n, peer in enumerate(col_peers)
    ][::-1] + outgoing
    for flag, copies in outgoing:

        @pl.when(flag)
        def _():
            copies[0].start()

    project(loads, small, emb, w, lens_ref, bias_ref, order, mine, owned, cells)

    for flag, copies in outgoing:

        @pl.when(flag)
        def _():
            copies[1].start()

    small[2].wait()
    small[3].wait()

    @pl.when(here)
    def _():
        merge_taps(conv_ref, bil, stack_w, width)
        row_buf[c] = mine[...]
        row_len[c] = my_len[...]

        @pl.when(my_block == c)
        def _():
            col_buf[my_slot] = mine[...]
            col_len[my_slot] = my_len[...]

        for d in range(1, cols):
            peer = lax.rem(c + cols - d, cols)
            for pair in (
                (row_len.at[peer], rl_recv.at[peer]),
                (row_buf.at[peer], row_recv.at[peer]),
            ):
                pltpu.make_async_copy(pair[0], pair[0], pair[1]).wait()

        fill_rows(row_buf, row_len, row_stack, owned, cells, width)

        for slot in range(rows):

            @pl.when(c * rows + slot != flat)
            def _():
                for pair in (
                    (col_len.at[slot], cl_recv.at[slot]),
                    (col_buf.at[slot], col_recv.at[slot]),
                ):
                    pltpu.make_async_copy(pair[0], pair[0], pair[1]).wait()

        high = GROUP * cells
        halves = cells // 8
        for chunk in range(rows * owned // GROUP):
            base = chunk * GROUP
            fill_cols(col_buf, col_len, base, stack_w, col_stack, folded, owned, cells, width)
            tiles = pair_tiles(row_stack, folded, cells)
            j_id = c * rows * owned + base + lax.broadcasted_iota(jnp.int32, (GROUP, high), 0)
            for i in range(GROUP):
                keep = j_id > r * cols * owned + i
                for half in range(halves):
                    out_ref[i, pl.ds(base, GROUP), half * high : (half + 1) * high] = jnp.where(
                        keep, tiles[i, half], 0.0
                    )

    @pl.when(jnp.logical_not(here))
    def _():
        out_ref[...] = jnp.zeros_like(out_ref)

    for flag, copies in outgoing:

        @pl.when(flag)
        def _():
            for copy in copies:
                copy.wait_send()


def shards(rows, cols, embeddings, proj_weight, proj_bias, bilinear, conv_kernel, lengths):
    owned, extent, embed = embeddings.shape
    width = proj_weight.shape[1]
    cells = extent // POOL
    assert owned * cols == GROUP and (owned * rows) % GROUP == 0
    assert extent == width == GROUP * cells
    bf16, f32 = jnp.bfloat16, jnp.float32
    dma = pltpu.SemaphoreType.DMA
    high = POOL * GROUP * cells
    loaded = [
        pltpu.VMEM((CHUNKS, owned * extent, embed // CHUNKS), bf16),
        pltpu.VMEM((CHUNKS, embed // CHUNKS, width), bf16),
        pltpu.VMEM(bilinear.shape, bf16),
        pltpu.SMEM((owned,), jnp.int32),
        pltpu.SMEM((3, conv_kernel.shape[0], 3), f32),
        pltpu.VMEM(proj_bias.shape, f32),
        pltpu.VMEM((owned * extent, owned * extent), bf16),
        pltpu.VMEM((POOL, owned, cells, width), bf16),
        pltpu.VMEM((8, width), jnp.int32),
    ]
    worked = [
        pltpu.VMEM((3 * width, 3 * width), bf16),
        pltpu.VMEM((high, 3 * width), bf16),
        pltpu.VMEM((high, 3 * width), bf16),
        pltpu.VMEM((high, 3 * width), bf16),
    ]
    out_shape = (owned * cols, owned * rows, cells * cells)
    if rows == cols and cols % 2 == 0:
        body = functools.partial(square_kernel, rows, owned, cells)
        scratch = (
            loaded
            + [
                pltpu.VMEM((2, cols, POOL, owned, cells, width), bf16),
                pltpu.VMEM((2, cols, 8, width), jnp.int32),
            ]
            + worked
            + [
                dma((2 * CHUNKS + 4,)),
                dma((cols,)),
                dma((cols,)),
                dma((2, cols)),
                dma((cols,)),
                dma((cols,)),
                dma((2, cols)),
                dma((cols,)),
            ]
        )
    else:
        body = functools.partial(kernel, rows, cols, owned, cells)
        scratch = (
            loaded
            + [
                pltpu.VMEM((cols, POOL, owned, cells, width), bf16),
                pltpu.VMEM((rows, POOL, owned, cells, width), bf16),
                pltpu.VMEM((cols, 8, width), jnp.int32),
                pltpu.VMEM((rows, 8, width), jnp.int32),
            ]
            + worked
            + [dma((2 * CHUNKS + 4,))]
            + [dma((n,)) for n in (cols, cols, rows, rows, cols, cols, rows, rows)]
        )
    return pl.pallas_call(
        body,
        out_shape=jax.ShapeDtypeStruct(out_shape, f32),
        in_specs=[pl.BlockSpec(memory_space=pl.ANY)] * 6,
        out_specs=pl.BlockSpec(memory_space=pltpu.VMEM),
        scratch_shapes=scratch,
        compiler_params=pltpu.CompilerParams(
            collective_id=0, has_side_effects=True, vmem_limit_bytes=63 * 1024 * 1024
        ),
    )(
        lengths,
        jnp.transpose(conv_kernel, (1, 0, 2)),
        proj_bias,
        bilinear,
        embeddings.reshape(owned * extent, embed),
        proj_weight,
    )


def solution(mesh):
    in_specs = (
        P(("groups", "row", "col"), None, None),
        P(),
        P(),
        P(),
        P(),
        P(("groups", "row", "col")),
    )
    out_specs = P(("groups", "row"), "col", None)
    body = functools.partial(shards, mesh.shape["row"], mesh.shape["col"])
    return jax.shard_map(body, mesh=mesh, in_specs=in_specs, out_specs=out_specs, check_vma=False)
```

```python
import functools

import jax
import jax.numpy as jnp
from jax import lax
from jax.experimental import pallas as pl
from jax.experimental.pallas import tpu as pltpu
from jax.sharding import PartitionSpec as P

POOL = 8
GROUP = 8
MESH = pl.DeviceIdType.MESH
CHUNKS = 2


def shifted(slab, step, cells):
    count = slab.shape[0]
    wide = slab.astype(jnp.float32)
    cell = lax.broadcasted_iota(jnp.int32, wide.shape, 0) % cells
    if step > 0:
        moved = jnp.where(cell == cells - 1, 0.0, pltpu.roll(wide, count - 1, 0))
    else:
        moved = jnp.where(cell == 0, 0.0, pltpu.roll(wide, 1, 0))
    return moved.astype(jnp.bfloat16)


def masks(lens, base, owned, cells, width):
    parts = []
    for i in range(GROUP):
        parts.append(
            jnp.broadcast_to(lens[(base + i) // owned, (base + i) % owned][None, :], (cells, width))
        )
    limits = jnp.concatenate(parts, axis=0)
    first = (lax.broadcasted_iota(jnp.int32, limits.shape, 0) % cells) * POOL
    return [jnp.where(first + k < limits, 1.0, 0.0) for k in range(POOL)]


def build(buf, base, k, cells, width):
    def slab(index):
        return buf[index, pl.ds(base, GROUP)].reshape(GROUP * cells, width)

    before = slab(k - 1) if k > 0 else shifted(slab(POOL - 1), -1, cells)
    after = slab(k + 1) if k < POOL - 1 else shifted(slab(0), 1, cells)
    return before, slab(k), after


def merge_taps(conv_ref, bil, stack_w, width):
    channels = conv_ref.shape[1]
    for u in range(3):
        for v in range(3):
            form = jnp.zeros((width, width), jnp.float32)
            for h in range(channels):
                form = form + (conv_ref[u, h, v] * width ** (-0.5)) * bil[
                    :, h * width : (h + 1) * width
                ].astype(jnp.float32)
            stack_w[v * width : (v + 1) * width, u * width : (u + 1) * width] = form.astype(jnp.bfloat16)


def fill_rows(buf, lens, row_stack, owned, cells, width):
    high = GROUP * cells
    row_mask = masks(lens, 0, owned, cells, width)
    for k in range(POOL):
        parts = build(buf, 0, k, cells, width)
        keep = row_mask[k].astype(jnp.bfloat16)
        for u in range(3):
            row_stack[k * high : (k + 1) * high, u * width : (u + 1) * width] = parts[u] * keep


def fill_cols(buf, lens, base, stack_w, col_stack, folded, owned, cells, width):
    high = GROUP * cells
    col_mask = masks(lens, base, owned, cells, width)
    for k in range(POOL):
        parts = build(buf, base, k, cells, width)
        for v in range(3):
            col_stack[k * high : (k + 1) * high, v * width : (v + 1) * width] = parts[v]
    for k in range(POOL):
        image = jnp.dot(
            col_stack[k * high : (k + 1) * high, :], stack_w[...], preferred_element_type=jnp.float32
        )
        keep = jnp.concatenate([col_mask[k]] * 3, axis=1)
        folded[k * high : (k + 1) * high, :] = (image * keep).astype(jnp.bfloat16)


def pair_tiles(row_stack, folded, cells):
    high = GROUP * cells
    best = None
    for step in range(POOL // 2):
        contact = lax.dot_general(
            row_stack[...],
            folded[step * 2 * high : (step + 1) * 2 * high, :],
            (((1,), (1,)), ((), ())),
            preferred_element_type=jnp.float32,
        )
        for k in range(POOL):
            for half in range(2):
                part = contact[k * high : (k + 1) * high, half * high : (half + 1) * high]
                best = part if best is None else jnp.maximum(best, part)
    sub = lax.broadcasted_iota(jnp.int32, best.shape, 0) % 8
    lane = lax.broadcasted_iota(jnp.int32, best.shape, 1) // cells
    for bit in (1, 2, 4):
        down = pltpu.roll(pltpu.roll(best, bit, 0), high - bit * cells, 1)
        up = pltpu.roll(pltpu.roll(best, high - bit, 0), bit * cells, 1)
        s_on = (sub & bit) != 0
        l_on = (lane & bit) != 0
        best = jnp.where(s_on == l_on, best, jnp.where(s_on, down, up))
    return best.reshape(GROUP, cells // 8, GROUP, high)


def start_loads(refs, load_sem):
    lens_hbm, conv_hbm, bias_hbm, bil_hbm, emb_hbm, w_hbm, emb, w, bil, lens_ref, conv_ref, bias_ref = refs
    small = [
        pltpu.make_async_copy(src, dst, load_sem.at[2 * CHUNKS + n])
        for n, (src, dst) in enumerate(
            ((lens_hbm, lens_ref), (bias_hbm, bias_ref), (bil_hbm, bil), (conv_hbm, conv_ref))
        )
    ]
    small[0].start()
    depth = emb_hbm.shape[1] // CHUNKS
    loads = []
    for n in range(CHUNKS):
        span = pl.ds(n * depth, depth)
        pair = (
            pltpu.make_async_copy(emb_hbm.at[:, span], emb.at[n], load_sem.at[2 * n]),
            pltpu.make_async_copy(w_hbm.at[span, :], w.at[n], load_sem.at[2 * n + 1]),
        )
        for copy in pair:
            copy.start()
        loads.append(pair)
    for copy in small[1:]:
        copy.start()
    return small, loads


def make_order(order, owned, cells):
    extent, size = cells * POOL, owned * cells * POOL
    to_row = lax.broadcasted_iota(jnp.int32, (size, size), 0)
    from_row = lax.broadcasted_iota(jnp.int32, (size, size), 1)
    k_of = to_row // (owned * cells)
    rest = to_row % (owned * cells)
    wanted = (rest // cells) * extent + (rest % cells) * POOL + k_of
    order[...] = jnp.where(wanted == from_row, 1.0, 0.0).astype(jnp.bfloat16)


def project(loads, small, emb, w, lens_ref, bias_ref, order, mine, owned, cells):
    f32, bf16 = jnp.float32, jnp.bfloat16
    extent, width = cells * POOL, w.shape[2]
    small[1].wait()
    total = jnp.zeros((owned * extent, width), f32)
    for n, pair in enumerate(loads):
        for copy in pair:
            copy.wait()
        total = total + jnp.dot(emb[n], w[n], preferred_element_type=f32)
    place = lax.broadcasted_iota(jnp.int32, (owned * extent, width), 0)
    limit = jnp.zeros((owned * extent, width), jnp.int32)
    for p in range(owned):
        limit = jnp.where(place // extent == p, lens_ref[p] + p * extent, limit)
    total = jnp.maximum(total + bias_ref[...][None, :], 0.0)
    residues = jnp.where(place < limit, total, 0.0).astype(bf16)
    ordered = jnp.dot(order[...], residues, preferred_element_type=f32).astype(bf16)
    mine[...] = ordered.reshape(POOL, owned, cells, width)


def fill_len(small, lens_ref, my_len, owned):
    small[0].wait()
    my_len[...] = jnp.zeros_like(my_len)
    for p in range(owned):
        my_len[p : p + 1, :] = jnp.full((1, my_len.shape[1]), lens_ref[p], jnp.int32)


ABOVE = ((1, 2),)


def square_kernel(
    size, owned, cells, lens_hbm, conv_hbm, bias_hbm, bil_hbm, emb_hbm, w_hbm, out_ref,
    emb, w, bil, lens_ref, conv_ref, bias_ref, order, mine, my_len, buf, lens,
    stack_w, row_stack, col_stack, folded, tiles, landing,
    load_sem, home_send, away_send, recv, len_home_send, len_away_send, len_recv, out_sem,
):
    width = bil.shape[0]
    g = lax.axis_index("groups")
    a = lax.axis_index("row")
    b = lax.axis_index("col")

    def above(r, c):
        flag = jnp.bool_(False)
        for x, y in ABOVE:
            flag = jnp.logical_or(flag, jnp.logical_and(r == x, c == y))
        return flag

    def active(row, col):
        below = jnp.logical_and(row < col, jnp.logical_not(above(row, col)))
        return jnp.logical_or(row == col, jnp.logical_or(below, jnp.logical_and(row > col, above(col, row))))

    def one(flag):
        return jnp.where(flag, 1, 0)

    here = active(a, b)
    gives = jnp.logical_and(a > b, here)
    takes = jnp.logical_and(a < b, jnp.logical_not(here))
    small, loads = start_loads(
        (lens_hbm, conv_hbm, bias_hbm, bil_hbm, emb_hbm, w_hbm, emb, w, bil, lens_ref, conv_ref, bias_ref),
        load_sem,
    )

    barrier = pltpu.get_barrier_semaphore()

    def greet(row, col):
        pl.semaphore_signal(barrier, inc=1, device_id=(g, row, col), device_id_type=MESH)

    homes = [lax.rem(b + d, size) for d in range(1, size)]
    aways = [lax.rem(a + d, size) for d in range(1, size)]

    @pl.when(here)
    def _():
        for peer in homes:
            greet(a, peer)

    @pl.when(jnp.logical_and(here, a != b))
    def _():
        for peer in range(size):
            greet(b, peer)

    @pl.when(takes)
    def _():
        greet(b, a)

    make_order(order, owned, cells)
    fill_len(small, lens_ref, my_len, owned)
    sends = one(gives)
    for peer in homes:
        sends = sends + one(active(a, peer))
    for peer in aways:
        sends = sends + one(active(peer, a))
    pl.semaphore_wait(barrier, sends)

    def copies(kind, n, row, col):
        to = dict(device_id=(g, row, col), device_id_type=MESH)
        return (
            pltpu.make_async_remote_copy(
                src_ref=my_len,
                dst_ref=lens.at[kind, b],
                send_sem=(len_home_send, len_away_send)[kind].at[n],
                recv_sem=len_recv.at[kind, b],
                **to,
            ),
            pltpu.make_async_remote_copy(
                src_ref=mine,
                dst_ref=buf.at[kind, :, pl.ds(b * owned, owned)],
                send_sem=(home_send, away_send)[kind].at[n],
                recv_sem=recv.at[kind, b],
                **to,
            ),
        )

    outgoing = [(active(peer, a), copies(1, n, peer, a)) for n, peer in enumerate(aways)]
    outgoing += [(active(a, peer), copies(0, n, a, peer)) for n, peer in enumerate(homes)]
    for flag, pair in outgoing:

        @pl.when(flag)
        def _():
            pair[0].start()

    project(loads, small, emb, w, lens_ref, bias_ref, order, mine, owned, cells)

    for flag, pair in outgoing:

        @pl.when(flag)
        def _():
            pair[1].start()

    small[2].wait()
    small[3].wait()

    def wait_for(kind):
        for source in range(size):

            @pl.when(jnp.logical_or(kind == 1, source != b))
            def _():
                for ref, sem in (
                    (lens.at[kind, source], len_recv.at[kind, source]),
                    (buf.at[kind, :, pl.ds(source * owned, owned)], recv.at[kind, source]),
                ):
                    pltpu.make_async_copy(ref, ref, sem).wait()

    answer = pltpu.make_async_remote_copy(
        src_ref=tiles,
        dst_ref=landing,
        send_sem=out_sem.at[0],
        recv_sem=out_sem.at[1],
        device_id=(g, b, a),
        device_id_type=MESH,
    )

    @pl.when(here)
    def _():
        merge_taps(conv_ref, bil, stack_w, width)
        buf[0, :, pl.ds(b * owned, owned)] = mine[...]
        lens[0, b] = my_len[...]
        row_kind = one(a > b)
        col_kind = one(a < b)
        wait_for(row_kind)
        fill_rows(buf.at[row_kind], lens.at[row_kind], row_stack, owned, cells, width)

        @pl.when(a != b)
        def _():
            wait_for(col_kind)

        fill_cols(
            buf.at[col_kind], lens.at[col_kind], 0, stack_w, col_stack, folded, owned, cells, width
        )
        found = pair_tiles(row_stack, folded, cells)
        halves, high = found.shape[1], found.shape[3]
        j_id = b * size * owned + lax.broadcasted_iota(jnp.int32, (GROUP, high), 0)
        for i in range(GROUP):
            keep = jnp.logical_or(j_id > a * size * owned + i, a != b)
            for half in range(halves):
                tile = jnp.where(keep, found[i, half], 0.0)
                tiles[i, :, half * high : (half + 1) * high] = tile

        @pl.when(gives)
        def _():
            answer.start()

    @pl.when(jnp.logical_and(here, a <= b))
    def _():
        out_ref[...] = tiles[...]

    @pl.when(a > b)
    def _():
        out_ref[...] = jnp.zeros_like(out_ref)

    @pl.when(takes)
    def _():
        answer.wait_recv()
        out_ref[...] = landing[...]

    for flag, pair in outgoing:

        @pl.when(flag)
        def _():
            for copy in pair:
                copy.wait_send()

    @pl.when(gives)
    def _():
        answer.wait_send()


def kernel(
    rows,
    cols,
    owned,
    cells,
    lens_hbm,
    conv_hbm,
    bias_hbm,
    bil_hbm,
    emb_hbm,
    w_hbm,
    out_ref,
    emb,
    w,
    bil,
    lens_ref,
    conv_ref,
    bias_ref,
    order,
    mine,
    my_len,
    row_buf,
    col_buf,
    row_len,
    col_len,
    stack_w,
    row_stack,
    col_stack,
    folded,
    load_sem,
    row_send,
    row_recv,
    col_send,
    col_recv,
    rl_send,
    rl_recv,
    cl_send,
    cl_recv,
):
    width = bil.shape[0]
    g = lax.axis_index("groups")
    r = lax.axis_index("row")
    c = lax.axis_index("col")
    flat = r * cols + c
    my_block = flat // rows
    my_slot = flat % rows

    def active(row, col):
        return (col + 1) * rows * owned > row * cols * owned + 1

    def one(flag):
        return jnp.where(flag, 1, 0)

    here = active(r, c)

    small, loads = start_loads(
        (lens_hbm, conv_hbm, bias_hbm, bil_hbm, emb_hbm, w_hbm, emb, w, bil, lens_ref, conv_ref, bias_ref),
        load_sem,
    )

    row_peers = [lax.rem(c + d, cols) for d in range(1, cols)]
    col_peers = [lax.rem(r + d, rows) for d in range(rows)]

    def col_remote(row):
        same = jnp.logical_and(row == r, my_block == c)
        return jnp.logical_and(active(row, my_block), jnp.logical_not(same))

    barrier = pltpu.get_barrier_semaphore()
    for peer in row_peers:

        @pl.when(here)
        def _():
            pl.semaphore_signal(barrier, inc=1, device_id=(g, r, peer), device_id_type=MESH)

    for slot in range(rows):
        source = c * rows + slot

        @pl.when(jnp.logical_and(here, source != flat))
        def _():
            pl.semaphore_signal(
                barrier, inc=1, device_id=(g, source // cols, source % cols), device_id_type=MESH
            )

    make_order(order, owned, cells)
    fill_len(small, lens_ref, my_len, owned)
    sends = 0
    for peer in row_peers:
        sends = sends + one(active(r, peer))
    for peer in col_peers:
        sends = sends + one(col_remote(peer))
    pl.semaphore_wait(barrier, sends)

    def row_copies(n, peer):
        to = dict(device_id=(g, r, peer), device_id_type=MESH)
        return (
            pltpu.make_async_remote_copy(
                src_ref=my_len, dst_ref=row_len.at[c], send_sem=rl_send.at[n], recv_sem=rl_recv.at[c], **to
            ),
            pltpu.make_async_remote_copy(
                src_ref=mine,
                dst_ref=row_buf.at[:, pl.ds(c * owned, owned)],
                send_sem=row_send.at[n],
                recv_sem=row_recv.at[c],
                **to,
            ),
        )

    def col_copies(n, peer):
        to = dict(device_id=(g, peer, my_block), device_id_type=MESH)
        return (
            pltpu.make_async_remote_copy(
                src_ref=my_len,
                dst_ref=col_len.at[my_slot],
                send_sem=cl_send.at[n],
                recv_sem=cl_recv.at[my_slot],
                **to,
            ),
            pltpu.make_async_remote_copy(
                src_ref=mine,
                dst_ref=col_buf.at[:, pl.ds(my_slot * owned, owned)],
                send_sem=col_send.at[n],
                recv_sem=col_recv.at[my_slot],
                **to,
            ),
        )

    outgoing = [(active(r, peer), row_copies(n, peer)) for n, peer in enumerate(row_peers)]
    outgoing = [
        (col_remote(peer), col_copies(n, peer)) for n, peer in enumerate(col_peers)
    ][::-1] + outgoing
    for flag, copies in outgoing:

        @pl.when(flag)
        def _():
            copies[0].start()

    project(loads, small, emb, w, lens_ref, bias_ref, order, mine, owned, cells)

    for flag, copies in outgoing:

        @pl.when(flag)
        def _():
            copies[1].start()

    small[2].wait()
    small[3].wait()

    @pl.when(here)
    def _():
        merge_taps(conv_ref, bil, stack_w, width)
        row_buf[:, pl.ds(c * owned, owned)] = mine[...]
        row_len[c] = my_len[...]

        @pl.when(my_block == c)
        def _():
            col_buf[:, pl.ds(my_slot * owned, owned)] = mine[...]
            col_len[my_slot] = my_len[...]

        for d in range(1, cols):
            peer = lax.rem(c + cols - d, cols)
            for pair in (
                (row_len.at[peer], rl_recv.at[peer]),
                (row_buf.at[:, pl.ds(peer * owned, owned)], row_recv.at[peer]),
            ):
                pltpu.make_async_copy(pair[0], pair[0], pair[1]).wait()

        fill_rows(row_buf, row_len, row_stack, owned, cells, width)

        for slot in range(rows):

            @pl.when(c * rows + slot != flat)
            def _():
                for pair in (
                    (col_len.at[slot], cl_recv.at[slot]),
                    (col_buf.at[:, pl.ds(slot * owned, owned)], col_recv.at[slot]),
                ):
                    pltpu.make_async_copy(pair[0], pair[0], pair[1]).wait()

        high = GROUP * cells
        halves = cells // 8
        for chunk in range(rows * owned // GROUP):
            base = chunk * GROUP
            fill_cols(col_buf, col_len, base, stack_w, col_stack, folded, owned, cells, width)
            tiles = pair_tiles(row_stack, folded, cells)
            j_id = c * rows * owned + base + lax.broadcasted_iota(jnp.int32, (GROUP, high), 0)
            for i in range(GROUP):
                keep = j_id > r * cols * owned + i
                for half in range(halves):
                    out_ref[i, pl.ds(base, GROUP), half * high : (half + 1) * high] = jnp.where(
                        keep, tiles[i, half], 0.0
                    )

    @pl.when(jnp.logical_not(here))
    def _():
        out_ref[...] = jnp.zeros_like(out_ref)

    for flag, copies in outgoing:

        @pl.when(flag)
        def _():
            for copy in copies:
                copy.wait_send()


def shards(rows, cols, embeddings, proj_weight, proj_bias, bilinear, conv_kernel, lengths):
    owned, extent, embed = embeddings.shape
    width = proj_weight.shape[1]
    cells = extent // POOL
    assert owned * cols == GROUP and (owned * rows) % GROUP == 0
    assert extent == width == GROUP * cells
    bf16, f32 = jnp.bfloat16, jnp.float32
    dma = pltpu.SemaphoreType.DMA
    high = POOL * GROUP * cells
    loaded = [
        pltpu.VMEM((CHUNKS, owned * extent, embed // CHUNKS), bf16),
        pltpu.VMEM((CHUNKS, embed // CHUNKS, width), bf16),
        pltpu.VMEM(bilinear.shape, bf16),
        pltpu.SMEM((owned,), jnp.int32),
        pltpu.SMEM((3, conv_kernel.shape[0], 3), f32),
        pltpu.VMEM(proj_bias.shape, f32),
        pltpu.VMEM((owned * extent, owned * extent), bf16),
        pltpu.VMEM((POOL, owned, cells, width), bf16),
        pltpu.VMEM((8, width), jnp.int32),
    ]
    worked = [
        pltpu.VMEM((3 * width, 3 * width), bf16),
        pltpu.VMEM((high, 3 * width), bf16),
        pltpu.VMEM((high, 3 * width), bf16),
        pltpu.VMEM((high, 3 * width), bf16),
    ]
    out_shape = (owned * cols, owned * rows, cells * cells)
    if rows == cols:
        body = functools.partial(square_kernel, rows, owned, cells)
        scratch = (
            loaded
            + [
                pltpu.VMEM((2, POOL, owned * cols, cells, width), bf16),
                pltpu.VMEM((2, cols, 8, width), jnp.int32),
            ]
            + worked
            + [pltpu.VMEM(out_shape, f32), pltpu.VMEM(out_shape, f32)]
            + [
                dma((2 * CHUNKS + 4,)),
                dma((cols,)),
                dma((cols,)),
                dma((2, cols)),
                dma((cols,)),
                dma((cols,)),
                dma((2, cols)),
                dma((2,)),
            ]
        )
    else:
        body = functools.partial(kernel, rows, cols, owned, cells)
        scratch = (
            loaded
            + [
                pltpu.VMEM((POOL, owned * cols, cells, width), bf16),
                pltpu.VMEM((POOL, owned * rows, cells, width), bf16),
                pltpu.VMEM((cols, 8, width), jnp.int32),
                pltpu.VMEM((rows, 8, width), jnp.int32),
            ]
            + worked
            + [dma((2 * CHUNKS + 4,))]
            + [dma((n,)) for n in (cols, cols, rows, rows, cols, cols, rows, rows)]
        )
    return pl.pallas_call(
        body,
        out_shape=jax.ShapeDtypeStruct(out_shape, f32),
        in_specs=[pl.BlockSpec(memory_space=pl.ANY)] * 6,
        out_specs=pl.BlockSpec(memory_space=pltpu.VMEM),
        scratch_shapes=scratch,
        compiler_params=pltpu.CompilerParams(
            collective_id=0, has_side_effects=True, vmem_limit_bytes=48 * 1024 * 1024
        ),
    )(
        *(
            pltpu.with_memory_space_constraint(operand, pltpu.HBM)
            for operand in (
                lengths,
                jnp.transpose(conv_kernel, (1, 0, 2)),
                proj_bias,
                bilinear,
                embeddings.reshape(owned * extent, embed),
                proj_weight,
            )
        )
    )


def solution(mesh):
    in_specs = (
        P(("groups", "row", "col"), None, None),
        P(),
        P(),
        P(),
        P(),
        P(("groups", "row", "col")),
    )
    out_specs = P(("groups", "row"), "col", None)
    body = functools.partial(shards, mesh.shape["row"], mesh.shape["col"])
    return jax.shard_map(body, mesh=mesh, in_specs=in_specs, out_specs=out_specs, check_vma=False)
```

```python
import functools

import jax
import jax.numpy as jnp
from jax import lax
from jax.experimental import pallas as pl
from jax.experimental.pallas import tpu as pltpu
from jax.sharding import PartitionSpec as P

POOL = 8
GROUP = 8
MESH = pl.DeviceIdType.MESH
CHUNKS = 1


def shifted(slab, step, cells):
    count = slab.shape[0]
    wide = slab.astype(jnp.float32)
    cell = lax.broadcasted_iota(jnp.int32, wide.shape, 0) % cells
    if step > 0:
        moved = jnp.where(cell == cells - 1, 0.0, pltpu.roll(wide, count - 1, 0))
    else:
        moved = jnp.where(cell == 0, 0.0, pltpu.roll(wide, 1, 0))
    return moved.astype(jnp.bfloat16)


def masks(lens, base, owned, cells, width):
    parts = []
    for i in range(GROUP):
        parts.append(
            jnp.broadcast_to(lens[(base + i) // owned, (base + i) % owned][None, :], (cells, width))
        )
    limits = jnp.concatenate(parts, axis=0)
    first = (lax.broadcasted_iota(jnp.int32, limits.shape, 0) % cells) * POOL
    return [jnp.where(first + k < limits, 1.0, 0.0) for k in range(POOL)]


def build(buf, base, k, cells, width):
    def slab(index):
        return buf[index, pl.ds(base, GROUP)].reshape(GROUP * cells, width)

    before = slab(k - 1) if k > 0 else shifted(slab(POOL - 1), -1, cells)
    after = slab(k + 1) if k < POOL - 1 else shifted(slab(0), 1, cells)
    return before, slab(k), after


def merge_taps(conv_ref, bil, stack_w, width):
    channels = conv_ref.shape[1]
    for u in range(3):
        for v in range(3):
            form = jnp.zeros((width, width), jnp.float32)
            for h in range(channels):
                form = form + (conv_ref[u, h, v] * width ** (-0.5)) * bil[
                    :, h * width : (h + 1) * width
                ].astype(jnp.float32)
            stack_w[v * width : (v + 1) * width, u * width : (u + 1) * width] = form.astype(jnp.bfloat16)


def fill_rows(buf, lens, row_stack, owned, cells, width):
    high = GROUP * cells
    row_mask = masks(lens, 0, owned, cells, width)
    for k in range(POOL):
        parts = build(buf, 0, k, cells, width)
        keep = row_mask[k].astype(jnp.bfloat16)
        for u in range(3):
            row_stack[k * high : (k + 1) * high, u * width : (u + 1) * width] = parts[u] * keep


def fill_cols(buf, lens, base, stack_w, col_stack, folded, owned, cells, width):
    high = GROUP * cells
    col_mask = masks(lens, base, owned, cells, width)
    for k in range(POOL):
        parts = build(buf, base, k, cells, width)
        for v in range(3):
            col_stack[k * high : (k + 1) * high, v * width : (v + 1) * width] = parts[v]
    image = jnp.dot(col_stack[...], stack_w[...], preferred_element_type=jnp.float32)
    for k in range(POOL):
        keep = jnp.concatenate([col_mask[k]] * 3, axis=1)
        part = image[k * high : (k + 1) * high, :]
        folded[k * high : (k + 1) * high, :] = (part * keep).astype(jnp.bfloat16)


def pair_tiles(row_stack, folded, cells):
    high = GROUP * cells
    best = None
    for step in range(POOL // 2):
        contact = lax.dot_general(
            row_stack[...],
            folded[step * 2 * high : (step + 1) * 2 * high, :],
            (((1,), (1,)), ((), ())),
            preferred_element_type=jnp.float32,
        )
        for k in range(POOL):
            for half in range(2):
                part = contact[k * high : (k + 1) * high, half * high : (half + 1) * high]
                best = part if best is None else jnp.maximum(best, part)
    sub = lax.broadcasted_iota(jnp.int32, best.shape, 0) % 8
    lane = lax.broadcasted_iota(jnp.int32, best.shape, 1) // cells
    for bit in (1, 2, 4):
        down = pltpu.roll(pltpu.roll(best, bit, 0), high - bit * cells, 1)
        up = pltpu.roll(pltpu.roll(best, high - bit, 0), bit * cells, 1)
        s_on = (sub & bit) != 0
        l_on = (lane & bit) != 0
        best = jnp.where(s_on == l_on, best, jnp.where(s_on, down, up))
    return best.reshape(GROUP, cells // 8, GROUP, high)


def start_loads(refs, load_sem):
    lens_hbm, conv_hbm, bias_hbm, bil_hbm, emb_hbm, w_hbm, emb, w, bil, lens_ref, conv_ref, bias_ref = refs
    small = [
        pltpu.make_async_copy(src, dst, load_sem.at[2 * CHUNKS + n])
        for n, (src, dst) in enumerate(
            ((lens_hbm, lens_ref), (bias_hbm, bias_ref), (bil_hbm, bil), (conv_hbm, conv_ref))
        )
    ]
    small[0].start()
    depth = emb_hbm.shape[1] // CHUNKS
    loads = []
    for n in range(CHUNKS):
        span = pl.ds(n * depth, depth)
        pair = (
            pltpu.make_async_copy(emb_hbm.at[:, span], emb.at[n], load_sem.at[2 * n]),
            pltpu.make_async_copy(w_hbm.at[span, :], w.at[n], load_sem.at[2 * n + 1]),
        )
        for copy in pair:
            copy.start()
        loads.append(pair)
    for copy in small[1:]:
        copy.start()
    return small, loads


def make_order(order, owned, cells):
    extent, size = cells * POOL, owned * cells * POOL
    to_row = lax.broadcasted_iota(jnp.int32, (size, size), 0)
    from_row = lax.broadcasted_iota(jnp.int32, (size, size), 1)
    k_of = to_row // (owned * cells)
    rest = to_row % (owned * cells)
    wanted = (rest // cells) * extent + (rest % cells) * POOL + k_of
    order[...] = jnp.where(wanted == from_row, 1.0, 0.0).astype(jnp.bfloat16)


def project(loads, small, emb, w, lens_ref, bias_ref, order, mine, owned, cells):
    f32, bf16 = jnp.float32, jnp.bfloat16
    extent, width = cells * POOL, w.shape[2]
    small[1].wait()
    total = jnp.zeros((owned * extent, width), f32)
    for n, pair in enumerate(loads):
        for copy in pair:
            copy.wait()
        total = total + jnp.dot(emb[n], w[n], preferred_element_type=f32)
    place = lax.broadcasted_iota(jnp.int32, (owned * extent, width), 0)
    limit = jnp.zeros((owned * extent, width), jnp.int32)
    for p in range(owned):
        limit = jnp.where(place // extent == p, lens_ref[p] + p * extent, limit)
    total = jnp.maximum(total + bias_ref[...][None, :], 0.0)
    residues = jnp.where(place < limit, total, 0.0).astype(bf16)
    ordered = jnp.dot(order[...], residues, preferred_element_type=f32).astype(bf16)
    mine[...] = ordered.reshape(POOL, owned, cells, width)


def fill_len(small, lens_ref, my_len, owned):
    small[0].wait()
    my_len[...] = jnp.zeros_like(my_len)
    for p in range(owned):
        my_len[p : p + 1, :] = jnp.full((1, my_len.shape[1]), lens_ref[p], jnp.int32)


ABOVE = ((1, 2),)


def square_kernel(
    size, owned, cells, lens_hbm, conv_hbm, bias_hbm, bil_hbm, emb_hbm, w_hbm, out_ref,
    emb, w, bil, lens_ref, conv_ref, bias_ref, order, mine, my_len, buf, lens,
    stack_w, row_stack, col_stack, folded, tiles, landing,
    load_sem, home_send, away_send, recv, len_home_send, len_away_send, len_recv, out_sem,
):
    width = bil.shape[0]
    g = lax.axis_index("groups")
    a = lax.axis_index("row")
    b = lax.axis_index("col")

    def above(r, c):
        flag = jnp.bool_(False)
        for x, y in ABOVE:
            flag = jnp.logical_or(flag, jnp.logical_and(r == x, c == y))
        return flag

    def active(row, col):
        below = jnp.logical_and(row < col, jnp.logical_not(above(row, col)))
        return jnp.logical_or(row == col, jnp.logical_or(below, jnp.logical_and(row > col, above(col, row))))

    def one(flag):
        return jnp.where(flag, 1, 0)

    here = active(a, b)
    gives = jnp.logical_and(a > b, here)
    takes = jnp.logical_and(a < b, jnp.logical_not(here))
    small, loads = start_loads(
        (lens_hbm, conv_hbm, bias_hbm, bil_hbm, emb_hbm, w_hbm, emb, w, bil, lens_ref, conv_ref, bias_ref),
        load_sem,
    )

    barrier = pltpu.get_barrier_semaphore()

    def greet(row, col):
        pl.semaphore_signal(barrier, inc=1, device_id=(g, row, col), device_id_type=MESH)

    homes = [lax.rem(b + d, size) for d in range(1, size)]
    aways = [lax.rem(a + d, size) for d in range(1, size)]

    @pl.when(here)
    def _():
        for peer in homes:
            greet(a, peer)

    @pl.when(jnp.logical_and(here, a != b))
    def _():
        for peer in range(size):
            greet(b, peer)

    @pl.when(takes)
    def _():
        greet(b, a)

    make_order(order, owned, cells)
    fill_len(small, lens_ref, my_len, owned)
    sends = one(gives)
    for peer in homes:
        sends = sends + one(active(a, peer))
    for peer in aways:
        sends = sends + one(active(peer, a))
    pl.semaphore_wait(barrier, sends)

    def copies(kind, n, row, col):
        to = dict(device_id=(g, row, col), device_id_type=MESH)
        return (
            pltpu.make_async_remote_copy(
                src_ref=my_len,
                dst_ref=lens.at[kind, b],
                send_sem=(len_home_send, len_away_send)[kind].at[n],
                recv_sem=len_recv.at[kind, b],
                **to,
            ),
            pltpu.make_async_remote_copy(
                src_ref=mine,
                dst_ref=buf.at[kind, :, pl.ds(b * owned, owned)],
                send_sem=(home_send, away_send)[kind].at[n],
                recv_sem=recv.at[kind, b],
                **to,
            ),
        )

    outgoing = [(active(peer, a), copies(1, n, peer, a)) for n, peer in enumerate(aways)]
    outgoing += [(active(a, peer), copies(0, n, a, peer)) for n, peer in enumerate(homes)]
    for flag, pair in outgoing:

        @pl.when(flag)
        def _():
            pair[0].start()

    project(loads, small, emb, w, lens_ref, bias_ref, order, mine, owned, cells)

    for flag, pair in outgoing:

        @pl.when(flag)
        def _():
            pair[1].start()

    small[2].wait()
    small[3].wait()

    def wait_for(kind):
        for source in range(size):

            @pl.when(jnp.logical_or(kind == 1, source != b))
            def _():
                for ref, sem in (
                    (lens.at[kind, source], len_recv.at[kind, source]),
                    (buf.at[kind, :, pl.ds(source * owned, owned)], recv.at[kind, source]),
                ):
                    pltpu.make_async_copy(ref, ref, sem).wait()

    answer = pltpu.make_async_remote_copy(
        src_ref=tiles,
        dst_ref=landing,
        send_sem=out_sem.at[0],
        recv_sem=out_sem.at[1],
        device_id=(g, b, a),
        device_id_type=MESH,
    )

    @pl.when(here)
    def _():
        merge_taps(conv_ref, bil, stack_w, width)
        buf[0, :, pl.ds(b * owned, owned)] = mine[...]
        lens[0, b] = my_len[...]
        row_kind = one(a > b)
        col_kind = one(a < b)
        wait_for(row_kind)
        fill_rows(buf.at[row_kind], lens.at[row_kind], row_stack, owned, cells, width)

        @pl.when(a != b)
        def _():
            wait_for(col_kind)

        fill_cols(
            buf.at[col_kind], lens.at[col_kind], 0, stack_w, col_stack, folded, owned, cells, width
        )
        found = pair_tiles(row_stack, folded, cells)
        halves, high = found.shape[1], found.shape[3]
        j_id = b * size * owned + lax.broadcasted_iota(jnp.int32, (GROUP, high), 0)
        for i in range(GROUP):
            keep = jnp.logical_or(j_id > a * size * owned + i, a != b)
            for half in range(halves):
                tile = jnp.where(keep, found[i, half], 0.0)
                out_ref[i, :, half * high : (half + 1) * high] = tile
                tiles[i, :, half * high : (half + 1) * high] = tile

        @pl.when(gives)
        def _():
            answer.start()

    @pl.when(a > b)
    def _():
        out_ref[...] = jnp.zeros_like(out_ref)

    @pl.when(takes)
    def _():
        answer.wait_recv()
        out_ref[...] = landing[...]

    for flag, pair in outgoing:

        @pl.when(flag)
        def _():
            for copy in pair:
                copy.wait_send()

    @pl.when(gives)
    def _():
        answer.wait_send()


def kernel(
    rows,
    cols,
    owned,
    cells,
    lens_hbm,
    conv_hbm,
    bias_hbm,
    bil_hbm,
    emb_hbm,
    w_hbm,
    out_ref,
    emb,
    w,
    bil,
    lens_ref,
    conv_ref,
    bias_ref,
    order,
    mine,
    my_len,
    row_buf,
    col_buf,
    row_len,
    col_len,
    stack_w,
    row_stack,
    col_stack,
    folded,
    load_sem,
    row_send,
    row_recv,
    col_send,
    col_recv,
    rl_send,
    rl_recv,
    cl_send,
    cl_recv,
):
    width = bil.shape[0]
    g = lax.axis_index("groups")
    r = lax.axis_index("row")
    c = lax.axis_index("col")
    flat = r * cols + c
    my_block = flat // rows
    my_slot = flat % rows

    def active(row, col):
        return (col + 1) * rows * owned > row * cols * owned + 1

    def one(flag):
        return jnp.where(flag, 1, 0)

    here = active(r, c)

    small, loads = start_loads(
        (lens_hbm, conv_hbm, bias_hbm, bil_hbm, emb_hbm, w_hbm, emb, w, bil, lens_ref, conv_ref, bias_ref),
        load_sem,
    )

    row_peers = [lax.rem(c + d, cols) for d in range(1, cols)]
    col_peers = [lax.rem(r + d, rows) for d in range(rows)]

    def col_remote(row):
        same = jnp.logical_and(row == r, my_block == c)
        return jnp.logical_and(active(row, my_block), jnp.logical_not(same))

    barrier = pltpu.get_barrier_semaphore()
    for peer in row_peers:

        @pl.when(here)
        def _():
            pl.semaphore_signal(barrier, inc=1, device_id=(g, r, peer), device_id_type=MESH)

    for slot in range(rows):
        source = c * rows + slot

        @pl.when(jnp.logical_and(here, source != flat))
        def _():
            pl.semaphore_signal(
                barrier, inc=1, device_id=(g, source // cols, source % cols), device_id_type=MESH
            )

    make_order(order, owned, cells)
    fill_len(small, lens_ref, my_len, owned)
    sends = 0
    for peer in row_peers:
        sends = sends + one(active(r, peer))
    for peer in col_peers:
        sends = sends + one(col_remote(peer))
    pl.semaphore_wait(barrier, sends)

    def row_copies(n, peer):
        to = dict(device_id=(g, r, peer), device_id_type=MESH)
        return (
            pltpu.make_async_remote_copy(
                src_ref=my_len, dst_ref=row_len.at[c], send_sem=rl_send.at[n], recv_sem=rl_recv.at[c], **to
            ),
            pltpu.make_async_remote_copy(
                src_ref=mine,
                dst_ref=row_buf.at[:, pl.ds(c * owned, owned)],
                send_sem=row_send.at[n],
                recv_sem=row_recv.at[c],
                **to,
            ),
        )

    def col_copies(n, peer):
        to = dict(device_id=(g, peer, my_block), device_id_type=MESH)
        return (
            pltpu.make_async_remote_copy(
                src_ref=my_len,
                dst_ref=col_len.at[my_slot],
                send_sem=cl_send.at[n],
                recv_sem=cl_recv.at[my_slot],
                **to,
            ),
            pltpu.make_async_remote_copy(
                src_ref=mine,
                dst_ref=col_buf.at[:, pl.ds(my_slot * owned, owned)],
                send_sem=col_send.at[n],
                recv_sem=col_recv.at[my_slot],
                **to,
            ),
        )

    outgoing = [(active(r, peer), row_copies(n, peer)) for n, peer in enumerate(row_peers)]
    outgoing = [
        (col_remote(peer), col_copies(n, peer)) for n, peer in enumerate(col_peers)
    ][::-1] + outgoing
    for flag, copies in outgoing:

        @pl.when(flag)
        def _():
            copies[0].start()

    project(loads, small, emb, w, lens_ref, bias_ref, order, mine, owned, cells)

    for flag, copies in outgoing:

        @pl.when(flag)
        def _():
            copies[1].start()

    small[2].wait()
    small[3].wait()

    @pl.when(here)
    def _():
        merge_taps(conv_ref, bil, stack_w, width)
        row_buf[:, pl.ds(c * owned, owned)] = mine[...]
        row_len[c] = my_len[...]

        @pl.when(my_block == c)
        def _():
            col_buf[:, pl.ds(my_slot * owned, owned)] = mine[...]
            col_len[my_slot] = my_len[...]

        for d in range(1, cols):
            peer = lax.rem(c + cols - d, cols)
            for pair in (
                (row_len.at[peer], rl_recv.at[peer]),
                (row_buf.at[:, pl.ds(peer * owned, owned)], row_recv.at[peer]),
            ):
                pltpu.make_async_copy(pair[0], pair[0], pair[1]).wait()

        fill_rows(row_buf, row_len, row_stack, owned, cells, width)

        for slot in range(rows):

            @pl.when(c * rows + slot != flat)
            def _():
                for pair in (
                    (col_len.at[slot], cl_recv.at[slot]),
                    (col_buf.at[:, pl.ds(slot * owned, owned)], col_recv.at[slot]),
                ):
                    pltpu.make_async_copy(pair[0], pair[0], pair[1]).wait()

        high = GROUP * cells
        halves = cells // 8
        for chunk in range(rows * owned // GROUP):
            base = chunk * GROUP
            fill_cols(col_buf, col_len, base, stack_w, col_stack, folded, owned, cells, width)
            tiles = pair_tiles(row_stack, folded, cells)
            j_id = c * rows * owned + base + lax.broadcasted_iota(jnp.int32, (GROUP, high), 0)
            for i in range(GROUP):
                keep = j_id > r * cols * owned + i
                for half in range(halves):
                    out_ref[i, pl.ds(base, GROUP), half * high : (half + 1) * high] = jnp.where(
                        keep, tiles[i, half], 0.0
                    )

    @pl.when(jnp.logical_not(here))
    def _():
        out_ref[...] = jnp.zeros_like(out_ref)

    for flag, copies in outgoing:

        @pl.when(flag)
        def _():
            for copy in copies:
                copy.wait_send()


def shards(rows, cols, embeddings, proj_weight, proj_bias, bilinear, conv_kernel, lengths):
    owned, extent, embed = embeddings.shape
    width = proj_weight.shape[1]
    cells = extent // POOL
    assert owned * cols == GROUP and (owned * rows) % GROUP == 0
    assert extent == width == GROUP * cells
    bf16, f32 = jnp.bfloat16, jnp.float32
    dma = pltpu.SemaphoreType.DMA
    high = POOL * GROUP * cells
    loaded = [
        pltpu.VMEM((CHUNKS, owned * extent, embed // CHUNKS), bf16),
        pltpu.VMEM((CHUNKS, embed // CHUNKS, width), bf16),
        pltpu.VMEM(bilinear.shape, bf16),
        pltpu.SMEM((owned,), jnp.int32),
        pltpu.SMEM((3, conv_kernel.shape[0], 3), f32),
        pltpu.VMEM(proj_bias.shape, f32),
        pltpu.VMEM((owned * extent, owned * extent), bf16),
        pltpu.VMEM((POOL, owned, cells, width), bf16),
        pltpu.VMEM((8, width), jnp.int32),
    ]
    worked = [
        pltpu.VMEM((3 * width, 3 * width), bf16),
        pltpu.VMEM((high, 3 * width), bf16),
        pltpu.VMEM((high, 3 * width), bf16),
        pltpu.VMEM((high, 3 * width), bf16),
    ]
    out_shape = (owned * cols, owned * rows, cells * cells)
    if rows == cols:
        body = functools.partial(square_kernel, rows, owned, cells)
        scratch = (
            loaded
            + [
                pltpu.VMEM((2, POOL, owned * cols, cells, width), bf16),
                pltpu.VMEM((2, cols, 8, width), jnp.int32),
            ]
            + worked
            + [pltpu.VMEM(out_shape, f32), pltpu.VMEM(out_shape, f32)]
            + [
                dma((2 * CHUNKS + 4,)),
                dma((cols,)),
                dma((cols,)),
                dma((2, cols)),
                dma((cols,)),
                dma((cols,)),
                dma((2, cols)),
                dma((2,)),
            ]
        )
    else:
        body = functools.partial(kernel, rows, cols, owned, cells)
        scratch = (
            loaded
            + [
                pltpu.VMEM((POOL, owned * cols, cells, width), bf16),
                pltpu.VMEM((POOL, owned * rows, cells, width), bf16),
                pltpu.VMEM((cols, 8, width), jnp.int32),
                pltpu.VMEM((rows, 8, width), jnp.int32),
            ]
            + worked
            + [dma((2 * CHUNKS + 4,))]
            + [dma((n,)) for n in (cols, cols, rows, rows, cols, cols, rows, rows)]
        )
    return pl.pallas_call(
        body,
        out_shape=jax.ShapeDtypeStruct(out_shape, f32),
        in_specs=[pl.BlockSpec(memory_space=pl.ANY)] * 6,
        out_specs=pl.BlockSpec(memory_space=pltpu.VMEM),
        scratch_shapes=scratch,
        compiler_params=pltpu.CompilerParams(
            collective_id=0, has_side_effects=True, vmem_limit_bytes=48 * 1024 * 1024
        ),
    )(
        *(
            pltpu.with_memory_space_constraint(operand, pltpu.HBM)
            for operand in (
                lengths,
                jnp.transpose(conv_kernel, (1, 0, 2)),
                proj_bias,
                bilinear,
                embeddings.reshape(owned * extent, embed),
                proj_weight,
            )
        )
    )


def solution(mesh):
    in_specs = (
        P(("groups", "row", "col"), None, None),
        P(),
        P(),
        P(),
        P(),
        P(("groups", "row", "col")),
    )
    out_specs = P(("groups", "row"), "col", None)
    body = functools.partial(shards, mesh.shape["row"], mesh.shape["col"])
    return jax.shard_map(body, mesh=mesh, in_specs=in_specs, out_specs=out_specs, check_vma=False)
```
